512 devices in a mesh: zero: 16 (over y, x), dp: 32 (over z, core).
Axes of the slice: x: 4, y: 4, z: 16, core: 2. Of those that a mesh axis runs over, the one named last changes fastest.
Arguments:
- hidden: bfloat16 [32, 4096, 1536], P('dp', 'zero'), may hold values from -6 to 6
- grad_out: bfloat16 [32, 4096, 4096], P('dp', 'zero'), may hold values from -0.015625 to 0.015625
- seed_table: int32 [32, 16, 1, 32], P('dp', 'zero'), may hold values from 0 to 8388607
Outputs:
- weight_grad: bfloat16 [1, 1536, 4096], P(None, 'zero')
The draws below stay inside these ranges and needn't reach their ends.
All inputs are finite; a program needn't handle non-finite values.
Results may differ from the reference program's by a relative error of at most 0.03.
Values may be sent and summed in bfloat16 or wider, within the bound.
No kernel may reach another device: no remote copies, remote signals or barrier semaphores. Data moves between devices by JAX's collectives and lax.ppermute only.
A program may use at most 128 MiB of HBM per device.

```python
import jax
import jax.numpy as jnp
import numpy as np
from jax import lax

DW = 4096
R = 1536
NB = 1
TOK = 256
SEEDS = 32
TOKENS_REPLICA = 4096
N_ZERO = 16
N_DP = 32


def place_ends(array, stream_key, smallest, largest):
    longest = array.shape.index(max(array.shape))
    spots = []
    for shift in (0, 1):
        where = [jax.random.randint(jax.random.fold_in(stream_key, axis), (), 0, length) for axis, length in enumerate(array.shape)]
        where[longest] = (where[longest] + shift) % array.shape[longest]
        spots.append(tuple(where))
    return array.at[spots[0]].set(smallest).at[spots[1]].set(largest)


def block_scale(rng, extent, pieces, low, high):
    def one(axis_at, shards_of):
        heights = jax.random.uniform(jax.random.fold_in(jax.random.fold_in(rng, 6), axis_at), (shards_of,), jnp.float32, low / len(pieces), high / len(pieces))
        return jnp.repeat(jnp.exp(heights), extent[axis_at] // shards_of).reshape((-1,) + (1,) * (len(extent) - axis_at - 1))

    gain = one(*pieces[0])
    for cut in pieces[1:]:
        gain = gain * one(*cut)
    return gain


def gaussian(key, shape, deviation, bound, shards=(), kind=jnp.bfloat16):
    gain = block_scale(key, shape, shards, -0.22, 0.18) if shards else 1.0
    values = jax.random.normal(key, shape, jnp.float32) * deviation * gain
    return jnp.minimum(jnp.maximum(values, -bound), bound).astype(kind)


def setup_inputs(seed: int = 0) -> dict:
    arg_keys = jax.random.split(jax.random.key(seed), 4)
    hidden = gaussian(arg_keys[0], (N_DP, TOKENS_REPLICA, NB * R), 1.0, 6.0, ((0, 32), (1, 16)))
    grad_out = gaussian(arg_keys[1], (N_DP, TOKENS_REPLICA, DW), (TOK * N_ZERO * N_DP) ** -0.5, 0.015625, ((0, 32), (1, 16)))
    seed_table = place_ends(jax.random.randint(arg_keys[2], (N_DP, N_ZERO, NB, SEEDS), 0, 8388608), jax.random.fold_in(arg_keys[2], 1), 0, 8388607).astype(jnp.int32)
    return {"hidden": hidden, "grad_out": grad_out, "seed_table": seed_table}


def scramble(hashed):
    hashed = hashed ^ lax.shift_right_logical(hashed, jnp.int32(16))
    hashed = hashed * jnp.int32(73244475)
    hashed = hashed ^ lax.shift_right_logical(hashed, jnp.int32(16))
    hashed = hashed * jnp.int32(73244475)
    hashed = hashed ^ lax.shift_right_logical(hashed, jnp.int32(16))
    return hashed


def dither_round(summed_pair, seed_row, row_start, step_no):
    row_total, feature_count = summed_pair.shape
    word_count = seed_row.shape[0]
    groups = feature_count // word_count
    row_ids = row_start + jnp.arange(row_total, dtype=jnp.int32)[:, None, None]
    group_ids = jnp.arange(groups, dtype=jnp.int32)[None, :, None]
    hashed = seed_row[None, None, :] + jnp.int32(131071) * row_ids + jnp.int32(65599) * group_ids + jnp.int32(7919 * step_no)
    hashed = scramble(hashed) & jnp.int32(65535)
    uniform_part = hashed.astype(jnp.float32) / 65536.0
    shaped = summed_pair.reshape(row_total, groups, word_count)
    dithered = shaped + shaped * ((uniform_part - 0.5) * (1.0 / 8.0))
    return dithered.reshape(row_total, feature_count).astype(jnp.bfloat16)


def reference(hidden, grad_out, seed_table):
    halving_steps = N_ZERO.bit_length() - 1
    owned_rows = R // N_ZERO
    zero_ids = np.arange(N_ZERO)

    def one_replica(carry, inputs):
        hidden_rep, grad_rep, seed_rep = inputs
        hidden_z = hidden_rep.reshape(N_ZERO, TOK, NB * R).astype(jnp.float32)
        grad_z = grad_rep.reshape(N_ZERO, TOK, DW).astype(jnp.float32)
        bucket_list = []
        for bucket in range(NB):
            local_grads = jnp.einsum("ztr,ztd->zrd", hidden_z[:, :, bucket * R:(bucket + 1) * R], grad_z)
            current = local_grads.astype(jnp.bfloat16)
            row_start = np.zeros(N_ZERO, dtype=np.int64)
            for step_no in range(halving_steps):
                bit_pos = halving_steps - 1 - step_no
                half_rows = current.shape[1] // 2
                upper_side = (zero_ids >> bit_pos) & 1
                partner = zero_ids ^ (1 << bit_pos)
                lower_half = current[:, :half_rows]
                upper_half = current[:, half_rows:]
                choose_upper = jnp.asarray(upper_side == 1)[:, None, None]
                kept_half = jnp.where(choose_upper, upper_half, lower_half)
                sent_half = jnp.where(choose_upper, lower_half, upper_half)
                received = sent_half[partner]
                row_start = row_start + upper_side * half_rows
                summed_pair = kept_half.astype(jnp.float32) + received.astype(jnp.float32)
                starts = jnp.asarray(row_start).astype(jnp.int32)
                current = jax.vmap(lambda pair_rows, seed_row, start_row: dither_round(pair_rows, seed_row, start_row, step_no))(summed_pair, seed_rep[:, bucket], starts)
            bucket_list.append(current)
        stacked = jnp.stack(bucket_list)
        return carry + stacked.astype(jnp.float32), None

    initial = jnp.zeros((NB, N_ZERO, owned_rows, DW), jnp.float32)
    summed, unused = lax.scan(one_replica, initial, (hidden, grad_out, seed_table))
    return summed.reshape(NB, R, DW).astype(jnp.bfloat16)
```

```python
import jax
import jax.numpy as jnp
from jax import lax
from jax.experimental import pallas as pl
from jax.experimental.pallas import tpu as pltpu
from jax.sharding import Mesh, PartitionSpec as P

SWAP = [(0, 1), (1, 0)]
MIX = 73244475
CHUNKS = 2


def factor(base, offset):
    k = base + offset
    k = k ^ lax.shift_right_logical(k, 16)
    k = k * MIX
    k = k ^ lax.shift_right_logical(k, 16)
    k = k * MIX
    k = (k ^ lax.shift_right_logical(k, 16)) & 65535
    return k.astype(jnp.float32) + 491520.0


def leaf_kernel(place, ha_ref, hb_ref, ga_ref, gb_ref, words_ref, out_ref, base_ref, *, tile):
    owner = pl.program_id(0)
    z, core, group0 = place[0], place[1], place[2]
    rows, width = out_ref.shape[1:]
    lane = lax.broadcasted_iota(jnp.int32, (8, 128), 1)
    sub = lax.broadcasted_iota(jnp.int32, (8, 128), 0)
    shared = 65599 * (lane >> 5) + 131071 * sub + (131071 * rows * owner + 65599 * group0)
    for rep in range(2):
        for step in range(4):
            low = 7 >> step
            keeper = (owner & (15 - low)) | (z & low)
            seeds = words_ref[pl.ds(keeper * 2 + (core ^ rep), 1), :]
            base_ref[rep, step] = seeds + shared + 7919 * step

    def columns(at, carry):
        first = pl.multiple_of(at * tile, tile)
        parts = [
            jnp.dot(h[...], g[:, pl.ds(first, tile)], preferred_element_type=jnp.float32)
            for h, g in ((ha_ref, ga_ref), (hb_ref, gb_ref))
        ]
        for row in range(0, rows, 16):
            for col in range(0, tile, 128):
                halves = []
                for top in (row, row + 8):
                    offset = (at * (tile // 128) + col // 128) * (4 * 65599) + 131071 * top
                    total = None
                    for rep in range(2):
                        f = [factor(base_ref[rep, step], offset) for step in range(4)]
                        scale = ((f[0] * f[1]) * (f[2] * f[3])) * (2.0**-76)
                        term = parts[rep][top : top + 8, col : col + 128] * scale
                        total = term if total is None else total + term
                    halves.append(total)
                block = jnp.concatenate(halves, axis=0).astype(jnp.bfloat16)
                out_ref[0, row : row + 16, pl.ds(pl.multiple_of(first + col, 128), 128)] = block
        return carry

    lax.fori_loop(0, width // tile, columns, 0)


def leaf(place, ha, hb, ga, gb, words, owners):
    rows_all, tokens = ha.shape
    width = ga.shape[1]
    rows = rows_all // owners
    tile = min(512, width)
    body = lambda *refs: leaf_kernel(*refs, tile=tile)
    return pl.pallas_call(
        body,
        grid_spec=pltpu.PrefetchScalarGridSpec(
            num_scalar_prefetch=1,
            grid=(owners,),
            in_specs=[
                pl.BlockSpec((rows, tokens), lambda i, p: (i, 0)),
                pl.BlockSpec((rows, tokens), lambda i, p: (i, 0)),
                pl.BlockSpec((tokens, width), lambda i, p: (0, 0)),
                pl.BlockSpec((tokens, width), lambda i, p: (0, 0)),
                pl.BlockSpec(words.shape, lambda i, p: (0, 0)),
            ],
            out_specs=pl.BlockSpec((1, rows, width), lambda i, p: (i, 0, 0)),
            scratch_shapes=[pltpu.VMEM((2, 4, 8, 128), jnp.int32)],
        ),
        out_shape=jax.ShapeDtypeStruct((owners, rows, width), jnp.bfloat16),
        compiler_params=pltpu.CompilerParams(vmem_limit_bytes=24 * 2**20),
        cost_estimate=pl.CostEstimate(
            flops=80 * rows_all * tokens * width, bytes_accessed=2 * rows_all * width * 2, transcendentals=0
        ),
    )(place, ha, hb, ga, gb, words)


def exchange(blocks, axes):
    return lax.all_to_all(blocks, axes, 0, 0, tiled=True)


def added(blocks):
    return jnp.sum(blocks.astype(jnp.float32), axis=0).astype(jnp.bfloat16)


def per_device(hidden, grad_out, seed_table):
    owners = lax.axis_size("y") * lax.axis_size("x")
    depth = lax.axis_size("z")
    core = lax.axis_index("core")
    z = lax.axis_index("y") * lax.axis_size("x") + lax.axis_index("x")
    h_own = hidden[0].T
    g_all = grad_out[0]
    half = g_all.shape[1] // 2
    h_other = lax.ppermute(h_own, "core", SWAP)
    g_own = lax.dynamic_slice_in_dim(g_all, core * half, half, 1)
    g_other = lax.ppermute(lax.dynamic_slice_in_dim(g_all, (1 - core) * half, half, 1), "core", SWAP)
    seeds = jnp.tile(seed_table[0, 0], (1, 4))
    words = exchange(jnp.broadcast_to(seeds, (2 * owners, 128)), ("y", "x", "core"))

    width = half // CHUNKS
    rows = h_own.shape[0] // owners
    across = min(depth, width // 128)
    down = depth // across
    mine = []
    for chunk in range(CHUNKS):
        place = jnp.stack([z, core, (core * half + chunk * width) // 32]).astype(jnp.int32)
        cut = slice(chunk * width, (chunk + 1) * width)
        partial = leaf(place, h_own, h_other, g_own[:, cut], g_other[:, cut], words, owners)
        owned = added(exchange(partial, ("y", "x")))
        cells = owned.reshape(down, rows // down, across, width // across).transpose(0, 2, 1, 3)
        cells = cells.reshape(depth, rows // down, width // across)
        cell = added(exchange(cells, "z"))
        everyone = exchange(jnp.broadcast_to(cell, cells.shape), "z")
        block = everyone.reshape(down, across, rows // down, width // across).transpose(0, 2, 1, 3)
        mine.append(block.reshape(rows, width))
    here = jnp.concatenate(mine, axis=1)
    there = lax.ppermute(here, "core", SWAP)
    first = core == 0
    result = jnp.concatenate([jnp.where(first, here, there), jnp.where(first, there, here)], axis=1)
    return result[None]


def solution(mesh):
    devices = mesh.devices
    zero, dp = devices.shape
    split = Mesh(devices.reshape(4, zero // 4, dp // 2, 2), ("y", "x", "z", "core"))
    return jax.shard_map(
        per_device,
        mesh=split,
        in_specs=(
            P(("z", "core"), ("y", "x"), None),
            P(("z", "core"), ("y", "x"), None),
            P(("z", "core"), ("y", "x"), None, None),
        ),
        out_specs=P(None, ("y", "x"), None),
        check_vma=False,
    )
```

```python
import functools

import jax
import jax.numpy as jnp
from jax import lax
from jax.experimental import pallas as pl
from jax.experimental.pallas import tpu as pltpu
from jax.sharding import Mesh, PartitionSpec as P

SWAP = [(0, 1), (1, 0)]
MIX = 73244475
SIDE = 4


def factor(base, offset):
    k = base + offset
    k = k ^ lax.shift_right_logical(k, 16)
    k = k * MIX
    k = k ^ lax.shift_right_logical(k, 16)
    k = k * MIX
    k = (k ^ lax.shift_right_logical(k, 16)) & 65535
    return k.astype(jnp.float32) + 491520.0


def column_kernel(place, h_ref, g_ref, words_ref, *refs, tile):
    more_ref, out_ref, base_ref = refs if len(refs) == 3 else (None, *refs)
    owner = pl.program_id(0)
    x, group0 = place[0], place[1]
    owner_y, owner_x = owner >> 2, owner & 3
    rows, width = out_ref.shape[2:]
    lane = lax.broadcasted_iota(jnp.int32, (8, 128), 1)
    sub = lax.broadcasted_iota(jnp.int32, (8, 128), 0)
    shared = 65599 * (lane >> 5) + 131071 * sub + (131071 * rows * owner + 65599 * group0)
    keepers = (
        ((owner_y & 2) * 4 + x, 0),
        (((owner_y & 2) | 1) * 4 + x, 0),
        (owner_y * 4 + x, 1),
        (owner_y * 4 + ((owner_x & 2) | (x & 1)), 2),
        (owner, 3),
    )
    for at, (keeper, step) in enumerate(keepers):
        base_ref[at] = words_ref[pl.ds(keeper, 1), :] + shared + 7919 * step

    def columns(at, carry):
        first = pl.multiple_of(at * tile, tile)

        def product(y):
            return jnp.dot(h_ref[y], g_ref[y, :, pl.ds(first, tile)], preferred_element_type=jnp.float32)

        pairs = [product(0) + product(2), product(1) + product(3)]
        for row in range(0, rows, 16):
            for col in range(0, tile, 128):
                halves = []
                for top in (row, row + 8):
                    offset = (at * (tile // 128) + col // 128) * (4 * 65599) + 131071 * top
                    f = [factor(base_ref[n], offset) for n in range(5)]
                    cut = (slice(top, top + 8), slice(col, col + 128))
                    summed = pairs[0][cut] * f[0] + pairs[1][cut] * f[1]
                    halves.append(summed * ((f[2] * (2.0**-38)) * ((f[3] * (2.0**-38)) * f[4])))
                block = jnp.concatenate(halves, axis=0)
                spot = (0, 0, slice(row, row + 16), pl.ds(pl.multiple_of(first + col, 128), 128))
                if more_ref is not None:
                    block = block + more_ref[spot].astype(jnp.float32)
                out_ref[spot] = block.astype(jnp.bfloat16)
        return carry

    lax.fori_loop(0, width // tile, columns, 0)


def column_part(place, h, g, words, more=None):
    sources, rows_all, tokens = h.shape
    width = g.shape[2] // 2
    owners = SIDE * SIDE
    rows = rows_all // owners
    body = functools.partial(column_kernel, tile=min(512, width))
    cell = pl.BlockSpec((1, 1, rows, width), lambda i, p: (i % SIDE, i // SIDE, 0, 0))
    specs = [
        pl.BlockSpec((sources, rows, tokens), lambda i, p: (0, i, 0)),
        pl.BlockSpec((sources, tokens, width), lambda i, p: (0, 0, p[2])),
        pl.BlockSpec(words.shape, lambda i, p: (0, 0)),
    ]
    args = [h, g, words]
    if more is not None:
        specs.append(cell)
        args.append(more)
    return pl.pallas_call(
        body,
        grid_spec=pltpu.PrefetchScalarGridSpec(
            num_scalar_prefetch=1,
            grid=(owners,),
            in_specs=specs,
            out_specs=cell,
            scratch_shapes=[pltpu.VMEM((5, 8, 128), jnp.int32)],
        ),
        out_shape=jax.ShapeDtypeStruct((SIDE, SIDE, rows, width), jnp.bfloat16),
        compiler_params=pltpu.CompilerParams(vmem_limit_bytes=24 * 2**20),
        cost_estimate=pl.CostEstimate(
            flops=2 * sources * rows_all * tokens * width, bytes_accessed=2 * rows_all * width * 2, transcendentals=0
        ),
    )(place, *args)


def exchange(blocks, axes):
    return lax.all_to_all(blocks, axes, 0, 0, tiled=True)


def added(blocks, axis=0):
    return jnp.sum(blocks.astype(jnp.float32), axis=axis).astype(jnp.bfloat16)


def per_device(hidden, grad_out, seed_table):
    depth = lax.axis_size("z")
    x, y, core = lax.axis_index("x"), lax.axis_index("y"), lax.axis_index("core")
    h = lax.all_gather(hidden[0].T, "y")
    tokens, columns = grad_out.shape[1:]
    quarter = columns // SIDE
    half = quarter // 2
    words = exchange(jnp.broadcast_to(jnp.tile(seed_table[0, 0], (1, 4)), (SIDE * SIDE, 128)), ("y", "x"))
    g = grad_out[0].reshape(tokens, SIDE, quarter).transpose(1, 0, 2)
    g, words = lax.optimization_barrier((g, words))
    g = exchange(g, "y")

    def place(which):
        return jnp.stack([x, (y * quarter + which * half) // 32, which]).astype(jnp.int32)

    sent = column_part(place(1 - core), h, g, words)
    received = lax.ppermute(sent, "core", SWAP)
    both = column_part(place(core), h, g, words, received)
    owned = added(exchange(both, "x"))

    rows = owned.shape[1]
    across = min(depth, half // 128, SIDE)
    down = depth // across
    cells = owned.reshape(SIDE, down, rows // down, across, half // across).transpose(0, 1, 3, 2, 4)
    cells = cells.reshape(SIDE * depth, rows // down, half // across)
    cells = exchange(cells, ("y", "z")).reshape(SIDE, depth, rows // down, half // across)
    cell = added(cells, 1)
    everyone = exchange(jnp.broadcast_to(cell, (depth, *cell.shape)), "z")
    here = everyone.reshape(down, across, SIDE, rows // down, half // across).transpose(0, 3, 2, 1, 4)
    here = here.reshape(rows, SIDE, half)
    there = lax.ppermute(here, "core", SWAP)
    first = core == 0
    result = jnp.stack([jnp.where(first, here, there), jnp.where(first, there, here)], axis=2)
    return result.reshape(1, rows, columns)


def solution(mesh):
    devices = mesh.devices
    zero, dp = devices.shape
    split = Mesh(devices.reshape(SIDE, zero // SIDE, dp // 2, 2), ("y", "x", "z", "core"))
    return jax.shard_map(
        per_device,
        mesh=split,
        in_specs=(
            P(("z", "core"), ("y", "x"), None),
            P(("z", "core"), ("y", "x"), None),
            P(("z", "core"), ("y", "x"), None, None),
        ),
        out_specs=P(None, ("y", "x"), None),
        check_vma=False,
    )
```

```python
import jax
import jax.numpy as jnp
from jax import lax
from jax.experimental import pallas as pl
from jax.experimental.pallas import tpu as pltpu
from jax.sharding import Mesh, PartitionSpec as P

SWAP = [(0, 1), (1, 0)]
MIX = 73244475
SIDE = 4
OWNERS = SIDE * SIDE


def factor(base, offset):
    k = base + offset
    k = k ^ lax.shift_right_logical(k, 16)
    k = k * MIX
    k = k ^ lax.shift_right_logical(k, 16)
    k = k * MIX
    k = (k ^ lax.shift_right_logical(k, 16)) & 65535
    return k.astype(jnp.float32) + 491520.0


def factor_kernel(place, words_ref, out_ref, base_ref, *, tile):
    owner = pl.program_id(0)
    x, y, group0 = place[0], place[1], place[2]
    owner_y, owner_x = owner >> 2, owner & 3
    rows, width = out_ref.shape[1:]
    lane = lax.broadcasted_iota(jnp.int32, (8, 128), 1)
    sub = lax.broadcasted_iota(jnp.int32, (8, 128), 0)
    shared = 65599 * (lane >> 5) + 131071 * sub + (131071 * rows * owner + 65599 * group0)
    keepers = (
        (((owner_y & 2) | (y & 1)) * 4 + x, 0),
        (((owner_y & 2) | (1 - (y & 1))) * 4 + x, 0),
        (owner_y * 4 + x, 1),
        (owner_y * 4 + ((owner_x & 2) | (x & 1)), 2),
        (owner, 3),
    )
    for at, (keeper, step) in enumerate(keepers):
        base_ref[at] = words_ref[pl.ds(keeper, 1), :] + shared + 7919 * step

    def columns(at, carry):
        first = pl.multiple_of(at * tile, tile)
        for row in range(0, rows, 16):
            for col in range(0, tile, 128):
                halves = ([], [])
                for top in (row, row + 8):
                    offset = (at * (tile // 128) + col // 128) * (4 * 65599) + 131071 * top
                    f = [factor(base_ref[n], offset) for n in range(5)]
                    later = (f[2] * (2.0**-38)) * ((f[3] * (2.0**-38)) * f[4])
                    for pair in range(2):
                        halves[pair].append(f[pair] * later - 1.0)
                for pair in range(2):
                    block = jnp.concatenate(halves[pair], axis=0).astype(jnp.bfloat16)
                    out_ref[pair, row : row + 16, pl.ds(pl.multiple_of(first + col, 128), 128)] = block
        return carry

    lax.fori_loop(0, width // tile, columns, 0)


def factors(place, words, rows_all, width):
    rows = rows_all // OWNERS

    def body(*refs):
        factor_kernel(*refs, tile=min(512, width))

    return pl.pallas_call(
        body,
        grid_spec=pltpu.PrefetchScalarGridSpec(
            num_scalar_prefetch=1,
            grid=(OWNERS,),
            in_specs=[pl.BlockSpec(words.shape, lambda i, p: (0, 0))],
            out_specs=pl.BlockSpec((2, rows, width), lambda i, p: (0, i, 0)),
            scratch_shapes=[pltpu.VMEM((5, 8, 128), jnp.int32)],
        ),
        out_shape=jax.ShapeDtypeStruct((2, rows_all, width), jnp.bfloat16),
        compiler_params=pltpu.CompilerParams(vmem_limit_bytes=8 * 2**20),
        cost_estimate=pl.CostEstimate(
            flops=1000 * rows_all * width * 10, bytes_accessed=2 * rows_all * width * 2, transcendentals=0
        ),
    )(place, words)


def pairs_kernel(place, h0, h2a, h2b, h1, h3, g0, g2, g1, g3, f_ref, *refs):
    more_ref, out_ref = refs if len(refs) == 2 else (None, *refs)

    def product(h, g):
        return jnp.dot(h, g[0], preferred_element_type=jnp.float32)

    facing = jnp.concatenate([h2a[...], h2b[...]], axis=1)
    near = product(h0[...], g0) + product(facing, g2)
    far = product(h1[...], g1) + product(h3[...], g3)
    total = near + near * f_ref[0].astype(jnp.float32) + (far + far * f_ref[1].astype(jnp.float32))
    if more_ref is not None:
        total = total + more_ref[...].astype(jnp.float32)
    out_ref[...] = total.astype(jnp.bfloat16)


def pairs(place, h, g, scale, more=None):
    rows_all, tokens = h[0].shape
    width = g.shape[2] // 2
    rows = rows_all // SIDE
    cell = pl.BlockSpec((rows, width), lambda i, p: (i, 0))

    def source(at):
        return pl.BlockSpec((1, tokens, width), lambda i, p: (p[at], 0, p[4]))

    specs = [pl.BlockSpec((rows, block.shape[1]), lambda i, p: (i, 0)) for block in h]
    specs += [source(0), source(2), source(1), source(3)]
    specs.append(pl.BlockSpec((2, rows, width), lambda i, p: (0, i, p[4])))
    args = [*h, g, g, g, g, scale]
    if more is not None:
        specs.append(cell)
        args.append(more)
    return pl.pallas_call(
        pairs_kernel,
        grid_spec=pltpu.PrefetchScalarGridSpec(num_scalar_prefetch=1, grid=(SIDE,), in_specs=specs, out_specs=cell),
        out_shape=jax.ShapeDtypeStruct((rows_all, width), jnp.bfloat16),
        compiler_params=pltpu.CompilerParams(vmem_limit_bytes=24 * 2**20),
        cost_estimate=pl.CostEstimate(
            flops=8 * rows_all * tokens * width, bytes_accessed=3 * rows_all * width * 2, transcendentals=0
        ),
    )(place, *args)


def exchange(blocks, axes):
    return lax.all_to_all(blocks, axes, 0, 0, tiled=True)


def added(blocks, axis=0):
    return jnp.sum(blocks.astype(jnp.float32), axis=axis).astype(jnp.bfloat16)


def along_y(block, step):
    return lax.ppermute(block, "y", [(at, (at + step) % SIDE) for at in range(SIDE)])


def per_device(hidden, grad_out, seed_table):
    depth = lax.axis_size("z")
    x, y, core = lax.axis_index("x"), lax.axis_index("y"), lax.axis_index("core")
    tokens, columns = grad_out.shape[1:]
    quarter = columns // SIDE
    half = quarter // 2
    words = exchange(jnp.broadcast_to(jnp.tile(seed_table[0, 0], (1, 4)), (OWNERS, 128)), ("y", "x"))

    h_own = hidden[0].T
    h_low = along_y(h_own, 1)
    h_high = along_y(h_own, -1)
    h_facing_a = along_y(h_low[:, : tokens // 2], 1)
    h_facing_b = along_y(h_high[:, tokens // 2 :], -1)
    h = [h_own, h_facing_a, h_facing_b, h_high, h_low]

    g = grad_out[0].reshape(tokens, SIDE, quarter).transpose(1, 0, 2)
    g, words = lax.optimization_barrier((g, words))
    g = exchange(g, "y")

    rows_all = h_own.shape[0]
    scale = factors(jnp.stack([x, y, y * quarter // 32]).astype(jnp.int32), words, rows_all, quarter)

    def place(which):
        return jnp.stack([y, (y + 1) % SIDE, (y + 2) % SIDE, (y + 3) % SIDE, which]).astype(jnp.int32)

    sent = pairs(place(1 - core), h, g, scale)
    received = lax.ppermute(sent, "core", SWAP)
    both = pairs(place(core), h, g, scale, received)

    rows = rows_all // OWNERS
    got = exchange(both.reshape(OWNERS, rows, half), ("y", "x"))
    owned = added(got.reshape(SIDE, SIDE, rows, half), 1)
    lanes = half // SIDE
    cells = owned.reshape(SIDE, rows, SIDE, lanes).transpose(0, 2, 1, 3).reshape(depth, OWNERS // depth, rows, lanes)
    cell = added(exchange(cells, "z"))
    everyone = exchange(jnp.broadcast_to(cell, cells.shape), "z")
    here = everyone.reshape(SIDE, SIDE, rows, lanes).transpose(2, 0, 1, 3).reshape(rows, SIDE, half)
    there = lax.ppermute(here, "core", SWAP)
    first = core == 0
    result = jnp.stack([jnp.where(first, here, there), jnp.where(first, there, here)], axis=2)
    return result.reshape(1, rows, columns)


def solution(mesh):
    devices = mesh.devices
    zero, dp = devices.shape
    split = Mesh(devices.reshape(SIDE, zero // SIDE, dp // 2, 2), ("y", "x", "z", "core"))
    return jax.shard_map(
        per_device,
        mesh=split,
        in_specs=(
            P(("z", "core"), ("y", "x"), None),
            P(("z", "core"), ("y", "x"), None),
            P(("z", "core"), ("y", "x"), None, None),
        ),
        out_specs=P(None, ("y", "x"), None),
        check_vma=False,
    )
```

```python
import jax
import jax.numpy as jnp
from jax import lax
from jax.experimental import pallas as pl
from jax.experimental.pallas import tpu as pltpu
from jax.sharding import Mesh, PartitionSpec as P

SWAP = [(0, 1), (1, 0)]
MIX = 73244475
SIDE = 4
OWNERS = SIDE * SIDE


def factor(base, offset):
    k = base + offset
    k = k ^ lax.shift_right_logical(k, 16)
    k = k * MIX
    k = k ^ lax.shift_right_logical(k, 16)
    k = k * MIX
    k = (k ^ lax.shift_right_logical(k, 16)) & 65535
    return k.astype(jnp.float32) + 491520.0


def factor_kernel(place, words_ref, out_ref, base_ref, *, tile):
    owner = pl.program_id(0)
    x, y, group0 = place[0], place[1], place[2]
    owner_y, owner_x = owner >> 2, owner & 3
    rows, width = out_ref.shape[1:]
    lane = lax.broadcasted_iota(jnp.int32, (8, 128), 1)
    sub = lax.broadcasted_iota(jnp.int32, (8, 128), 0)
    shared = 65599 * (lane >> 5) + 131071 * sub + (131071 * rows * owner + 65599 * group0)
    keepers = (
        (((owner_y & 2) | (y & 1)) * 4 + x, 0),
        (((owner_y & 2) | (1 - (y & 1))) * 4 + x, 0),
        (owner_y * 4 + x, 1),
        (owner_y * 4 + ((owner_x & 2) | (x & 1)), 2),
        (owner, 3),
    )
    for at, (keeper, step) in enumerate(keepers):
        base_ref[at] = words_ref[pl.ds(keeper, 1), :] + shared + 7919 * step

    def columns(at, carry):
        first = pl.multiple_of(at * tile, tile)
        for row in range(0, rows, 16):
            for col in range(0, tile, 128):
                halves = ([], [])
                for top in (row, row + 8):
                    offset = (at * (tile // 128) + col // 128) * (4 * 65599) + 131071 * top
                    f = [factor(base_ref[n], offset) for n in range(5)]
                    later = (f[2] * (2.0**-38)) * ((f[3] * (2.0**-38)) * f[4])
                    for pair in range(2):
                        halves[pair].append(f[pair] * later - 1.0)
                for pair in range(2):
                    block = jnp.concatenate(halves[pair], axis=0).astype(jnp.bfloat16)
                    out_ref[pair, row : row + 16, pl.ds(pl.multiple_of(first + col, 128), 128)] = block
        return carry

    lax.fori_loop(0, width // tile, columns, 0)


def factors(place, words, rows_all, width):
    rows = rows_all // OWNERS

    def body(*refs):
        factor_kernel(*refs, tile=min(512, width))

    return pl.pallas_call(
        body,
        grid_spec=pltpu.PrefetchScalarGridSpec(
            num_scalar_prefetch=1,
            grid=(OWNERS,),
            in_specs=[pl.BlockSpec(words.shape, lambda i, p: (0, 0))],
            out_specs=pl.BlockSpec((2, rows, width), lambda i, p: (0, i, 0)),
            scratch_shapes=[pltpu.VMEM((5, 8, 128), jnp.int32)],
        ),
        out_shape=jax.ShapeDtypeStruct((2, rows_all, width), jnp.bfloat16),
        compiler_params=pltpu.CompilerParams(vmem_limit_bytes=8 * 2**20),
        cost_estimate=pl.CostEstimate(
            flops=1000 * rows_all * width * 10, bytes_accessed=2 * rows_all * width * 2, transcendentals=0
        ),
    )(place, words)


def pairs_kernel(place, h0, h2a, h2b, h1, h3, g0, g2, g1, g3, f_ref, out_ref):
    def product(left, right):
        left = jnp.concatenate([part[...] for part in left], axis=1)
        right = jnp.concatenate([part[0] for part in right], axis=0)
        return jnp.dot(left, right, preferred_element_type=jnp.float32)

    near = product((h0, h2a, h2b), (g0, g2))
    far = product((h1, h3), (g1, g3))
    total = near + near * f_ref[0].astype(jnp.float32) + (far + far * f_ref[1].astype(jnp.float32))
    out_ref[...] = total.astype(jnp.bfloat16)


def pairs(place, h, g, scale):
    rows_all, tokens = h[0].shape
    width = g.shape[2] // 2
    rows = rows_all // SIDE
    cell = pl.BlockSpec((rows, width), lambda i, p: (i, 0))

    def source(at):
        return pl.BlockSpec((1, tokens, width), lambda i, p: (p[at], 0, p[4]))

    specs = [pl.BlockSpec((rows, block.shape[1]), lambda i, p: (i, 0)) for block in h]
    specs += [source(0), source(2), source(1), source(3)]
    specs.append(pl.BlockSpec((2, rows, width), lambda i, p: (0, i, p[4])))
    return pl.pallas_call(
        pairs_kernel,
        grid_spec=pltpu.PrefetchScalarGridSpec(num_scalar_prefetch=1, grid=(SIDE,), in_specs=specs, out_specs=cell),
        out_shape=jax.ShapeDtypeStruct((rows_all, width), jnp.bfloat16),
        compiler_params=pltpu.CompilerParams(vmem_limit_bytes=56 * 2**20),
        cost_estimate=pl.CostEstimate(
            flops=8 * rows_all * tokens * width, bytes_accessed=3 * rows_all * width * 2, transcendentals=0
        ),
    )(place, *h, g, g, g, g, scale)


def exchange(blocks, axes):
    return lax.all_to_all(blocks, axes, 0, 0, tiled=True)


def added(blocks, axis=0):
    return jnp.sum(blocks.astype(jnp.float32), axis=axis).astype(jnp.bfloat16)


def along_y(block, step):
    return lax.ppermute(block, "y", [(at, (at + step) % SIDE) for at in range(SIDE)])


def per_device(hidden, grad_out, seed_table):
    depth = lax.axis_size("z")
    x, y, core = lax.axis_index("x"), lax.axis_index("y"), lax.axis_index("core")
    tokens, columns = grad_out.shape[1:]
    quarter = columns // SIDE
    half = quarter // 2
    words = exchange(jnp.broadcast_to(jnp.tile(seed_table[0, 0], (1, 4)), (OWNERS, 128)), ("y", "x"))

    h_own = hidden[0].T
    h_low = along_y(h_own, 1)
    h_high = along_y(h_own, -1)
    h_facing_a = along_y(h_low[:, : tokens // 2], 1)
    h_facing_b = along_y(h_high[:, tokens // 2 :], -1)
    h = [h_own, h_facing_a, h_facing_b, h_high, h_low]

    g = grad_out[0].reshape(tokens, SIDE, quarter).transpose(1, 0, 2)
    g, words = lax.optimization_barrier((g, words))
    g = exchange(g, "y")

    rows_all = h_own.shape[0]
    scale = factors(jnp.stack([x, y, y * quarter // 32]).astype(jnp.int32), words, rows_all, quarter)

    def place(which):
        return jnp.stack([y, (y + 1) % SIDE, (y + 2) % SIDE, (y + 3) % SIDE, which]).astype(jnp.int32)

    sent = pairs(place(1 - core), h, g, scale)
    received = lax.ppermute(sent, "core", SWAP)
    both = pairs(place(core), h, g, scale).astype(jnp.float32) + received.astype(jnp.float32)
    both = both.astype(jnp.bfloat16)

    rows = rows_all // OWNERS
    got = exchange(both.reshape(OWNERS, rows, half), ("y", "x"))
    owned = added(got.reshape(SIDE, SIDE, rows, half), 1)
    lanes = half // SIDE
    cells = owned.reshape(SIDE, rows, SIDE, lanes).transpose(0, 2, 1, 3).reshape(depth, OWNERS // depth, rows, lanes)
    cell = added(exchange(cells, "z"))
    everyone = exchange(jnp.broadcast_to(cell, cells.shape), "z")
    here = everyone.reshape(SIDE, SIDE, rows, lanes).transpose(2, 0, 1, 3).reshape(rows, SIDE, half)
    there = lax.ppermute(here, "core", SWAP)
    first = core == 0
    result = jnp.stack([jnp.where(first, here, there), jnp.where(first, there, here)], axis=2)
    return result.reshape(1, rows, columns)


def solution(mesh):
    devices = mesh.devices
    zero, dp = devices.shape
    split = Mesh(devices.reshape(SIDE, zero // SIDE, dp // 2, 2), ("y", "x", "z", "core"))
    return jax.shard_map(
        per_device,
        mesh=split,
        in_specs=(
            P(("z", "core"), ("y", "x"), None),
            P(("z", "core"), ("y", "x"), None),
            P(("z", "core"), ("y", "x"), None, None),
        ),
        out_specs=P(None, ("y", "x"), None),
        check_vma=False,
    )
```

```python
import jax
import jax.numpy as jnp
from jax import lax
from jax.experimental import pallas as pl
from jax.experimental.pallas import tpu as pltpu
from jax.sharding import Mesh, PartitionSpec as P

SWAP = [(0, 1), (1, 0)]
MIX = 73244475
SIDE = 4
OWNERS = SIDE * SIDE


def factor(base, offset):
    k = base + offset
    k = k ^ lax.shift_right_logical(k, 16)
    k = k * MIX
    k = k ^ lax.shift_right_logical(k, 16)
    k = k * MIX
    k = (k ^ lax.shift_right_logical(k, 16)) & 65535
    return k.astype(jnp.float32) + 491520.0


def factor_kernel(place, words_ref, out_ref, base_ref, *, tile, part):
    owner = pl.program_id(0)
    x, y, group0 = place[0], place[1], place[2 + part]
    owner_y, owner_x = owner >> 2, owner & 3
    rows, width = out_ref.shape[1:]
    lane = lax.broadcasted_iota(jnp.int32, (8, 128), 1)
    sub = lax.broadcasted_iota(jnp.int32, (8, 128), 0)
    shared = 65599 * (lane >> 5) + 131071 * sub + (131071 * rows * owner + 65599 * group0)
    keepers = (
        (((owner_y & 2) | (y & 1)) * 4 + x, 0),
        (((owner_y & 2) | (1 - (y & 1))) * 4 + x, 0),
        (owner_y * 4 + x, 1),
        (owner_y * 4 + ((owner_x & 2) | (x & 1)), 2),
        (owner, 3),
    )
    for at, (keeper, step) in enumerate(keepers):
        base_ref[at] = words_ref[pl.ds(keeper, 1), :] + shared + 7919 * step

    def columns(at, carry):
        first = pl.multiple_of(at * tile, tile)
        for row in range(0, rows, 16):
            for col in range(0, tile, 128):
                halves = ([], [])
                for top in (row, row + 8):
                    offset = (at * (tile // 128) + col // 128) * (4 * 65599) + 131071 * top
                    f = [factor(base_ref[n], offset) for n in range(5)]
                    later = (f[2] * (2.0**-38)) * ((f[3] * (2.0**-38)) * f[4])
                    for pair in range(2):
                        halves[pair].append(f[pair] * later - 1.0)
                for pair in range(2):
                    block = jnp.concatenate(halves[pair], axis=0).astype(jnp.bfloat16)
                    out_ref[pair, row : row + 16, pl.ds(pl.multiple_of(first + col, 128), 128)] = block
        return carry

    lax.fori_loop(0, width // tile, columns, 0)


def factors(place, words, rows_all, width, part):
    rows = rows_all // OWNERS

    def body(*refs):
        factor_kernel(*refs, tile=min(512, width), part=part)

    return pl.pallas_call(
        body,
        grid_spec=pltpu.PrefetchScalarGridSpec(
            num_scalar_prefetch=1,
            grid=(OWNERS,),
            in_specs=[pl.BlockSpec(words.shape, lambda i, p: (0, 0))],
            out_specs=pl.BlockSpec((2, rows, width), lambda i, p: (0, i, 0)),
            scratch_shapes=[pltpu.VMEM((5, 8, 128), jnp.int32)],
        ),
        out_shape=jax.ShapeDtypeStruct((2, rows_all, width), jnp.bfloat16),
        compiler_params=pltpu.CompilerParams(vmem_limit_bytes=8 * 2**20),
        cost_estimate=pl.CostEstimate(
            flops=10000 * rows_all * width, bytes_accessed=2 * rows_all * width * 2, transcendentals=0
        ),
    )(place, words)


def pairs_kernel(place, h0, h2a, h2b, h1, h3, g0, g2, g1, g3, f_ref, out_ref):
    def product(left, right):
        left = jnp.concatenate([part[...] for part in left], axis=1)
        right = jnp.concatenate([part[...] for part in right], axis=0)
        return jnp.dot(left, right, preferred_element_type=jnp.float32)

    near = product((h0, h2a, h2b), (g0, g2))
    far = product((h1, h3), (g1, g3))
    total = near + near * f_ref[0].astype(jnp.float32) + (far + far * f_ref[1].astype(jnp.float32))
    out_ref[...] = total.astype(jnp.bfloat16)


def pairs(place, h, g, scale, part):
    rows_all, tokens = h[0].shape
    width = scale.shape[2]
    rows = rows_all // SIDE
    specs = [pl.BlockSpec((rows, block.shape[1]), lambda i, p: (i, 0)) for block in h]
    specs.append(pl.BlockSpec((tokens, width), lambda i, p: (0, p[4 + part])))
    specs += [pl.BlockSpec((tokens, width), lambda i, p: (0, p[6 + part]))] * 3
    specs.append(pl.BlockSpec((2, rows, width), lambda i, p: (0, i, 0)))
    return pl.pallas_call(
        pairs_kernel,
        grid_spec=pltpu.PrefetchScalarGridSpec(
            num_scalar_prefetch=1,
            grid=(SIDE,),
            in_specs=specs,
            out_specs=pl.BlockSpec((rows, width), lambda i, p: (i, 0)),
        ),
        out_shape=jax.ShapeDtypeStruct((rows_all, width), jnp.bfloat16),
        compiler_params=pltpu.CompilerParams(vmem_limit_bytes=16 * 2**20),
        cost_estimate=pl.CostEstimate(
            flops=8 * rows_all * tokens * width, bytes_accessed=3 * rows_all * width * 2, transcendentals=0
        ),
    )(place, *h, *g, scale)


def weave_kernel(place, here_ref, there_ref, out_ref):
    width = here_ref.shape[2]
    first = place[7] == 0
    here, there = here_ref[0], there_ref[0]
    out_ref[:, :width] = jnp.where(first, here, there)
    out_ref[:, width:] = jnp.where(first, there, here)


def weave(place, here, there):
    sides, rows, width = here.shape
    cell = pl.BlockSpec((1, rows, width), lambda i, p: (i, 0, 0))
    return pl.pallas_call(
        weave_kernel,
        grid_spec=pltpu.PrefetchScalarGridSpec(
            num_scalar_prefetch=1,
            grid=(sides,),
            in_specs=[cell, cell],
            out_specs=pl.BlockSpec((rows, 2 * width), lambda i, p: (0, i)),
        ),
        out_shape=jax.ShapeDtypeStruct((rows, sides * 2 * width), here.dtype),
        compiler_params=pltpu.CompilerParams(vmem_limit_bytes=8 * 2**20),
    )(place, here, there)


def exchange(blocks, axes):
    return lax.all_to_all(blocks, axes, 0, 0, tiled=True)


def added(blocks, axis=0):
    return jnp.sum(blocks.astype(jnp.float32), axis=axis).astype(jnp.bfloat16)


def along_y(block, step):
    return lax.ppermute(block, "y", [(at, (at + step) % SIDE) for at in range(SIDE)])


def per_device(hidden, grad_out, seed_table):
    depth = lax.axis_size("zh")
    x, y, core = lax.axis_index("x"), lax.axis_index("y"), lax.axis_index("core")
    tokens, columns = grad_out.shape[1:]
    quarter = columns // SIDE
    half = quarter // 2
    words = exchange(jnp.broadcast_to(jnp.tile(seed_table[0, 0], (1, 4)), (OWNERS, 128)), ("y", "x"))
    other = 1 - core
    groups = half // 32
    place = [x, y, (y * 2 + other) * groups, (y * 2 + core) * groups, y * 2 + other, y * 2 + core, other, core]
    place = jnp.stack(place).astype(jnp.int32)

    h_own = hidden[0].T
    h_low = along_y(h_own, 1)
    h_high = along_y(h_own, -1)
    h_facing_a = along_y(h_low[:, : tokens // 2], 1)
    h_facing_b = along_y(h_high[:, tokens // 2 :], -1)
    h = [h_own, h_facing_a, h_facing_b, h_high, h_low]

    def quarter_for(step):
        return lax.dynamic_slice_in_dim(grad_out[0], (y + step) % SIDE * quarter, quarter, 1)

    g_low, g_high, g_facing = (along_y(quarter_for(step), step) for step in (1, -1, 2))
    g = [grad_out[0], g_facing, g_high, g_low]

    rows_all = h_own.shape[0]
    scale = [factors(place, words, rows_all, half, part) for part in range(2)]
    sent = pairs(place, h, g, scale[0], 0)
    received = lax.ppermute(sent, "core", SWAP)
    both = pairs(place, h, g, scale[1], 1).astype(jnp.float32) + received.astype(jnp.float32)

    rows = rows_all // OWNERS
    got = exchange(both.astype(jnp.bfloat16).reshape(OWNERS, rows, half), ("y", "x"))
    owned = added(got.reshape(SIDE, SIDE, rows, half), 1)
    near = added(exchange(owned, "zl"))
    total = added(exchange(jnp.broadcast_to(near, (depth, *near.shape)), "zh"))
    here = lax.all_gather(total, "zl")
    there = lax.ppermute(here, "core", SWAP)
    return weave(place, here, there)[None]


def solution(mesh):
    devices = mesh.devices
    zero, dp = devices.shape
    split = Mesh(devices.reshape(SIDE, zero // SIDE, dp // 2 // SIDE, SIDE, 2), ("y", "x", "zh", "zl", "core"))
    return jax.shard_map(
        per_device,
        mesh=split,
        in_specs=(
            P(("zh", "zl", "core"), ("y", "x"), None),
            P(("zh", "zl", "core"), ("y", "x"), None),
            P(("zh", "zl", "core"), ("y", "x"), None, None),
        ),
        out_specs=P(None, ("y", "x"), None),
        check_vma=False,
    )
```

```python
import jax
import jax.numpy as jnp
from jax import lax
from jax.experimental import pallas as pl
from jax.experimental.pallas import tpu as pltpu
from jax.sharding import Mesh, PartitionSpec as P

SWAP = [(0, 1), (1, 0)]
MIX = 73244475
SIDE = 4
OWNERS = SIDE * SIDE


def factor(base, offset):
    k = base + offset
    k = k ^ lax.shift_right_logical(k, 16)
    k = k * MIX
    k = k ^ lax.shift_right_logical(k, 16)
    k = k * MIX
    k = (k ^ lax.shift_right_logical(k, 16)) & 65535
    return k.astype(jnp.float32) + 491520.0


def factor_kernel(place, words_ref, *refs):
    outs, base_ref = refs[:2], refs[2]
    owner = pl.program_id(0)
    x, y = place[0], place[1]
    owner_y, owner_x = owner >> 2, owner & 3
    rows, width = outs[0].shape[1:]
    lane = lax.broadcasted_iota(jnp.int32, (8, 128), 1)
    sub = lax.broadcasted_iota(jnp.int32, (8, 128), 0)
    shared = 65599 * (lane >> 5) + 131071 * sub + 131071 * rows * owner
    keepers = (
        (((owner_y & 2) | (y & 1)) * 4 + x, 0),
        (((owner_y & 2) | (1 - (y & 1))) * 4 + x, 0),
        (owner_y * 4 + x, 1),
        (owner_y * 4 + ((owner_x & 2) | (x & 1)), 2),
        (owner, 3),
    )
    for at, (keeper, step) in enumerate(keepers):
        base_ref[at] = words_ref[pl.ds(keeper, 1), :] + shared + 7919 * step

    def fill(out_ref, group0):
        for row in range(0, rows, 16):
            for col in range(0, width, 128):
                halves = ([], [])
                for top in (row, row + 8):
                    offset = 65599 * (group0 + col // 32) + 131071 * top
                    f = [factor(base_ref[n], offset) for n in range(5)]
                    later = (f[2] * (2.0**-38)) * ((f[3] * (2.0**-38)) * f[4])
                    for pair in range(2):
                        halves[pair].append(f[pair] * later - 1.0)
                for pair in range(2):
                    block = jnp.concatenate(halves[pair], axis=0).astype(jnp.bfloat16)
                    out_ref[pair, row : row + 16, col : col + 128] = block

    for part in range(2):
        fill(outs[part], place[2 + part])


def factors(place, words, rows_all, width):
    rows = rows_all // OWNERS
    spec = pl.BlockSpec((2, rows, width), lambda i, p: (0, i, 0))
    shape = jax.ShapeDtypeStruct((2, rows_all, width), jnp.bfloat16)
    return pl.pallas_call(
        factor_kernel,
        grid_spec=pltpu.PrefetchScalarGridSpec(
            num_scalar_prefetch=1,
            grid=(OWNERS,),
            in_specs=[pl.BlockSpec(words.shape, lambda i, p: (0, 0))],
            out_specs=[spec, spec],
            scratch_shapes=[pltpu.VMEM((5, 8, 128), jnp.int32)],
        ),
        out_shape=[shape, shape],
        compiler_params=pltpu.CompilerParams(vmem_limit_bytes=8 * 2**20),
        cost_estimate=pl.CostEstimate(
            flops=20000 * rows_all * width, bytes_accessed=4 * rows_all * width * 2, transcendentals=0
        ),
    )(place, words)


def pairs_kernel(place, h0, h2a, h2b, h1, h3, g0, g2, g1, g3, f_ref, out_ref, *, part):
    rows_all, width = out_ref.shape
    rows = rows_all // SIDE
    first = pl.multiple_of(place[6 + part] * width, width)

    def right(parts):
        return jnp.concatenate([ref[:, pl.ds(first, width)] for ref in parts], axis=0)

    sides = (((h0, h2a, h2b), (g0, g2)), ((h1, h3), (g1, g3)))

    def block(at, carry):
        here = pl.ds(pl.multiple_of(at * rows, rows), rows)
        total = None
        for pair, (left, own) in enumerate(sides):
            left = jnp.concatenate([ref[here, :] for ref in left], axis=1)
            value = jnp.dot(left, right(own), preferred_element_type=jnp.float32)
            value = value + value * f_ref[pair, here, :].astype(jnp.float32)
            total = value if total is None else total + value
        out_ref[here, :] = total.astype(jnp.bfloat16)
        return carry

    lax.fori_loop(0, SIDE, block, 0)


def pairs(place, h, g, scale, part):
    rows_all, tokens = h[0].shape
    width = scale.shape[2]

    def body(*refs):
        pairs_kernel(*refs, part=part)

    return pl.pallas_call(
        body,
        in_specs=[pl.BlockSpec(memory_space=pltpu.SMEM)] + [pl.BlockSpec(memory_space=pltpu.VMEM)] * (len(h) + len(g) + 1),
        out_specs=pl.BlockSpec(memory_space=pltpu.VMEM),
        out_shape=jax.ShapeDtypeStruct((rows_all, width), jnp.bfloat16),
        compiler_params=pltpu.CompilerParams(vmem_limit_bytes=24 * 2**20),
        cost_estimate=pl.CostEstimate(
            flops=8 * rows_all * tokens * width, bytes_accessed=3 * rows_all * width * 2, transcendentals=0
        ),
    )(place, *h, *g, scale)


def weave_kernel(place, here_ref, there_ref, out_ref):
    width = here_ref.shape[2]
    first = place[7] == 0
    here, there = here_ref[0], there_ref[0]
    out_ref[:, :width] = jnp.where(first, here, there)
    out_ref[:, width:] = jnp.where(first, there, here)


def weave(place, here, there):
    sides, rows, width = here.shape
    cell = pl.BlockSpec((1, rows, width), lambda i, p: (i, 0, 0))
    return pl.pallas_call(
        weave_kernel,
        grid_spec=pltpu.PrefetchScalarGridSpec(
            num_scalar_prefetch=1,
            grid=(sides,),
            in_specs=[cell, cell],
            out_specs=pl.BlockSpec((rows, 2 * width), lambda i, p: (0, i)),
        ),
        out_shape=jax.ShapeDtypeStruct((rows, sides * 2 * width), here.dtype),
        compiler_params=pltpu.CompilerParams(vmem_limit_bytes=8 * 2**20),
    )(place, here, there)


def exchange(blocks, axes):
    return lax.all_to_all(blocks, axes, 0, 0, tiled=True)


def added(blocks, axis=0):
    return jnp.sum(blocks.astype(jnp.float32), axis=axis).astype(jnp.bfloat16)


def along_y(block, step):
    return lax.ppermute(block, "y", [(at, (at + step) % SIDE) for at in range(SIDE)])


def per_device(hidden, grad_out, seed_table):
    x, y, core = lax.axis_index("x"), lax.axis_index("y"), lax.axis_index("core")
    tokens, columns = grad_out.shape[1:]
    quarter = columns // SIDE
    half = quarter // 2
    words = exchange(jnp.broadcast_to(jnp.tile(seed_table[0, 0], (1, 4)), (OWNERS, 128)), ("y", "x"))
    other = 1 - core
    groups = half // 32
    place = [x, y, (y * 2 + other) * groups, (y * 2 + core) * groups, y * 2 + other, y * 2 + core, other, core]
    place = jnp.stack(place).astype(jnp.int32)

    h_own = hidden[0].T
    h_low = along_y(h_own, 1)
    h_high = along_y(h_own, -1)
    h_facing_a = along_y(h_low[:, : tokens // 2], 1)
    h_facing_b = along_y(h_high[:, tokens // 2 :], -1)
    h = [h_own, h_facing_a, h_facing_b, h_high, h_low]

    def quarter_for(step):
        return lax.dynamic_slice_in_dim(grad_out[0], (y + step) % SIDE * quarter, quarter, 1)

    g_low, g_high, g_facing = (along_y(quarter_for(step), step) for step in (1, -1, 2))
    g = [quarter_for(0), g_facing, g_high, g_low]

    rows_all = h_own.shape[0]
    scale = factors(place, words, rows_all, half)
    sent = pairs(place, h, g, scale[0], 0)
    received = lax.ppermute(sent, "core", SWAP)
    both = pairs(place, h, g, scale[1], 1).astype(jnp.float32) + received.astype(jnp.float32)

    rows = rows_all // OWNERS
    got = exchange(both.astype(jnp.bfloat16).reshape(OWNERS, rows, half), ("y", "x"))
    owned = added(got.reshape(SIDE, SIDE, rows, half), 1)
    near = added(exchange(owned, "zl"))
    total = added(lax.all_gather(near, "zh"))
    here = lax.all_gather(total, "zl")
    there = lax.ppermute(here, "core", SWAP)
    return weave(place, here, there)[None]


def solution(mesh):
    devices = mesh.devices
    zero, dp = devices.shape
    split = Mesh(devices.reshape(SIDE, zero // SIDE, dp // 2 // SIDE, SIDE, 2), ("y", "x", "zh", "zl", "core"))
    return jax.shard_map(
        per_device,
        mesh=split,
        in_specs=(
            P(("zh", "zl", "core"), ("y", "x"), None),
            P(("zh", "zl", "core"), ("y", "x"), None),
            P(("zh", "zl", "core"), ("y", "x"), None, None),
        ),
        out_specs=P(None, ("y", "x"), None),
        check_vma=False,
    )
```

```python
import itertools

import jax
import jax.numpy as jnp
from jax import lax
from jax.experimental import pallas as pl
from jax.experimental.pallas import tpu as pltpu
from jax.sharding import Mesh, PartitionSpec as P

SWAP = [(0, 1), (1, 0)]
MIX = 73244475
SIDE = 4
OWNERS = SIDE * SIDE


def factor(base, offset):
    k = base + offset
    k = k ^ lax.shift_right_logical(k, 16)
    k = k * MIX
    k = k ^ lax.shift_right_logical(k, 16)
    k = k * MIX
    k = (k ^ lax.shift_right_logical(k, 16)) & 65535
    return k.astype(jnp.float32) + 491520.0


def factor_kernel(place, words_ref, *refs):
    outs, base_ref = refs[:2], refs[2]
    owner = pl.program_id(0)
    x, y = place[0], place[1]
    owner_y, owner_x = owner >> 2, owner & 3
    rows, width = outs[0].shape[1:]
    lane = lax.broadcasted_iota(jnp.int32, (8, 128), 1)
    sub = lax.broadcasted_iota(jnp.int32, (8, 128), 0)
    shared = 65599 * (lane >> 5) + 131071 * sub + 131071 * rows * owner
    keepers = (
        (((owner_y & 2) | (y & 1)) * 4 + x, 0),
        (((owner_y & 2) | (1 - (y & 1))) * 4 + x, 0),
        (owner_y * 4 + x, 1),
        (owner_y * 4 + ((owner_x & 2) | (x & 1)), 2),
        (owner, 3),
    )
    for at, (keeper, step) in enumerate(keepers):
        base_ref[at] = words_ref[pl.ds(keeper, 1), :] + shared + 7919 * step

    def fill(out_ref, group0):
        for row in range(0, rows, 16):
            for col in range(0, width, 128):
                halves = ([], [])
                for top in (row, row + 8):
                    offset = 65599 * (group0 + col // 32) + 131071 * top
                    f = [factor(base_ref[n], offset) for n in range(5)]
                    later = (f[2] * f[3] * f[4]) * (2.0**-76)
                    for pair in range(2):
                        halves[pair].append(f[pair] * later - 1.0)
                for pair in range(2):
                    block = jnp.concatenate(halves[pair], axis=0).astype(jnp.bfloat16)
                    out_ref[pair, row : row + 16, col : col + 128] = block

    for part in range(2):
        fill(outs[part], place[2 + part])


def factors(place, words, rows_all, width):
    rows = rows_all // OWNERS
    spec = pl.BlockSpec((2, rows, width), lambda i, p: (0, i, 0))
    shape = jax.ShapeDtypeStruct((2, rows_all, width), jnp.bfloat16)
    return pl.pallas_call(
        factor_kernel,
        grid_spec=pltpu.PrefetchScalarGridSpec(
            num_scalar_prefetch=1,
            grid=(OWNERS,),
            in_specs=[pl.BlockSpec(words.shape, lambda i, p: (0, 0))],
            out_specs=[spec, spec],
            scratch_shapes=[pltpu.VMEM((5, 8, 128), jnp.int32)],
        ),
        out_shape=[shape, shape],
        compiler_params=pltpu.CompilerParams(vmem_limit_bytes=8 * 2**20),
        cost_estimate=pl.CostEstimate(
            flops=20000 * rows_all * width, bytes_accessed=4 * rows_all * width * 2, transcendentals=0
        ),
    )(place, words)


def product(left, right):
    return jnp.dot(left, right, preferred_element_type=jnp.float32)


def early_kernel(place, h0, h1, h3, g0, g1, g3, fa_ref, fb_ref, outa_ref, outb_ref):
    rows_all, width = outa_ref.shape
    rows = rows_all // SIDE

    def block(at, carry):
        here = pl.ds(pl.multiple_of(at * rows, rows), rows)
        both = jnp.concatenate([h1[here, :], h3[here, :]], axis=1)
        for part, (f_ref, out_ref) in enumerate(((fa_ref, outa_ref), (fb_ref, outb_ref))):
            cut = pl.ds(pl.multiple_of(place[6 + part] * width, width), width)
            near = product(h0[here, :], g0[:, cut])
            far = product(both, jnp.concatenate([g1[:, cut], g3[:, cut]], axis=0))
            near = near + near * f_ref[0, here, :].astype(jnp.float32)
            out_ref[here, :] = near + (far + far * f_ref[1, here, :].astype(jnp.float32))
        return carry

    lax.fori_loop(0, SIDE, block, 0)


def late_kernel(place, h2a, h2b, g2, f_ref, more_ref, out_ref, *, part):
    rows_all, width = more_ref.shape
    rows = rows_all // SIDE
    cell_rows, cell_width = out_ref.shape[1:]
    cut = pl.ds(pl.multiple_of(place[6 + part] * width, width), width)

    def block(at, carry):
        here = pl.ds(pl.multiple_of(at * rows, rows), rows)
        left = jnp.concatenate([h2a[here, :], h2b[here, :]], axis=1)
        value = product(left, g2[:, cut])
        value = value + value * f_ref[0, here, :].astype(jnp.float32) + more_ref[here, :]
        value = value.astype(jnp.bfloat16)
        for x in range(SIDE):
            for side in range(2):
                cell = value[x * cell_rows : (x + 1) * cell_rows, side * cell_width : (side + 1) * cell_width]
                out_ref[(at * SIDE + x) * 2 + side] = cell
        return carry

    lax.fori_loop(0, SIDE, block, 0)


def in_vmem(body, place, args, shape, flops):
    return pl.pallas_call(
        body,
        in_specs=[pl.BlockSpec(memory_space=pltpu.SMEM)] + [pl.BlockSpec(memory_space=pltpu.VMEM)] * len(args),
        out_specs=jax.tree.map(lambda _: pl.BlockSpec(memory_space=pltpu.VMEM), shape),
        out_shape=shape,
        compiler_params=pltpu.CompilerParams(vmem_limit_bytes=24 * 2**20),
        cost_estimate=pl.CostEstimate(flops=flops, bytes_accessed=2**22, transcendentals=0),
    )(place, *args)


def early(place, h, g, scale):
    rows_all, tokens = h[0].shape
    width = scale[0].shape[2]
    shape = jax.ShapeDtypeStruct((rows_all, width), jnp.float32)
    return in_vmem(early_kernel, place, [*h, *g, *scale], [shape, shape], 12 * rows_all * tokens * width)


def late(place, h, g, scale, more, part):
    rows_all, width = more.shape

    def body(*refs):
        late_kernel(*refs, part=part)

    shape = jax.ShapeDtypeStruct((2 * OWNERS, rows_all // OWNERS, width // 2), jnp.bfloat16)
    return in_vmem(body, place, [*h, g, scale, more], shape, 8 * rows_all * g.shape[0] * width)


def weave_kernel(place, blocks_ref, out_ref):
    width = blocks_ref.shape[3]
    for z1, z0, core, low in itertools.product(range(2), repeat=4):
        first = (((z1 * 2 + low) * 2 + core) * 2 + z0) * width
        out_ref[:, first : first + width] = blocks_ref[z1 * 4 + z0 * 2 + core, low]


def weave(place, blocks, columns):
    rows, width = blocks.shape[2:]
    shape = jax.ShapeDtypeStruct((rows, columns), blocks.dtype)
    return in_vmem(weave_kernel, place, [blocks], shape, 1)


def exchange(blocks, axes):
    return lax.all_to_all(blocks, axes, 0, 0, tiled=True)


def added(blocks, axis=0):
    return jnp.sum(blocks.astype(jnp.float32), axis=axis).astype(jnp.bfloat16)


def along_y(block, step):
    return lax.ppermute(block, "y", [(at, (at + step) % SIDE) for at in range(SIDE)])


def per_device(hidden, grad_out, seed_table):
    x, y, core = lax.axis_index("x"), lax.axis_index("y"), lax.axis_index("core")
    tokens, columns = grad_out.shape[1:]
    quarter = columns // SIDE
    half = quarter // 2
    words = exchange(jnp.tile(seed_table[0, 0], (OWNERS, 4)), ("y", "x"))
    other = 1 - core
    groups = half // 32
    place = [x, y, (y * 2 + other) * groups, (y * 2 + core) * groups, y * 2 + other, y * 2 + core, other, core]
    place = jnp.stack(place).astype(jnp.int32)

    h_own = hidden[0].T
    h_low = along_y(h_own, 1)
    h_high = along_y(h_own, -1)
    h_facing_a = along_y(h_low[:, : tokens // 2], 1)
    h_facing_b = along_y(h_high[:, tokens // 2 :], -1)
    def quarter_for(step):
        return lax.dynamic_slice_in_dim(grad_out[0], (y + step) % SIDE * quarter, quarter, 1)

    g_low, g_high, g_facing = (along_y(quarter_for(step), step) for step in (1, -1, 2))

    rows_all = h_own.shape[0]
    scale = factors(place, words, rows_all, half)
    three = early(place, [h_own, h_high, h_low], [quarter_for(0), g_high, g_low], scale)
    facing = [h_facing_a, h_facing_b]
    sent = late(place, facing, g_facing, scale[0], three[0], 0)
    received = lax.ppermute(sent, "core", SWAP)
    both = late(place, facing, g_facing, scale[1], three[1], 1).astype(jnp.float32) + received.astype(jnp.float32)

    got = exchange(both.astype(jnp.bfloat16), ("y", "x", "z0"))
    owned = added(got.reshape(SIDE, 2 * SIDE, *got.shape[1:]), 1)
    near = added(exchange(owned, "z1").reshape(2, 2, *got.shape[1:]))
    total = added(lax.all_gather(near, "zh"))
    return weave(place, lax.all_gather(total, ("z1", "z0", "core")), columns)[None]


def solution(mesh):
    devices = mesh.devices
    zero, dp = devices.shape
    names = ("y", "x", "zh", "z1", "z0", "core")
    split = Mesh(devices.reshape(SIDE, zero // SIDE, dp // 8, 2, 2, 2), names)
    dp_parts = ("zh", "z1", "z0", "core")
    return jax.shard_map(
        per_device,
        mesh=split,
        in_specs=(
            P(dp_parts, ("y", "x"), None),
            P(dp_parts, ("y", "x"), None),
            P(dp_parts, ("y", "x"), None, None),
        ),
        out_specs=P(None, ("y", "x"), None),
        check_vma=False,
    )
```

```python
import itertools

import jax
import jax.numpy as jnp
from jax import lax
from jax.experimental import pallas as pl
from jax.experimental.pallas import tpu as pltpu
from jax.sharding import Mesh, PartitionSpec as P

SWAP = [(0, 1), (1, 0)]
MIX = 73244475
SIDE = 4
OWNERS = SIDE * SIDE


def factor(base, offset):
    k = base + offset
    k = k ^ lax.shift_right_logical(k, 16)
    k = k * MIX
    k = k ^ lax.shift_right_logical(k, 16)
    k = k * MIX
    k = (k ^ lax.shift_right_logical(k, 16)) & 65535
    return k.astype(jnp.float32) + 491520.0


def factor_kernel(place, words_ref, *refs):
    outs, base_ref = refs[:2], refs[2]
    owner = pl.program_id(0)
    x, y = place[0], place[1]
    owner_y, owner_x = owner >> 2, owner & 3
    rows, width = outs[0].shape[1:]
    lane = lax.broadcasted_iota(jnp.int32, (8, 128), 1)
    sub = lax.broadcasted_iota(jnp.int32, (8, 128), 0)
    shared = 65599 * (lane >> 5) + 131071 * sub + 131071 * rows * owner
    keepers = (
        (((owner_y & 2) | (y & 1)) * 4 + x, 0),
        (((owner_y & 2) | (1 - (y & 1))) * 4 + x, 0),
        (owner_y * 4 + x, 1),
        (owner_y * 4 + ((owner_x & 2) | (x & 1)), 2),
        (owner, 3),
    )
    for at, (keeper, step) in enumerate(keepers):
        base = words_ref[pl.ds(keeper, 1), :] + shared + 7919 * step
        for part in range(2):
            base_ref[part, at] = base + 65599 * place[2 + part]

    def fill(out_ref, bases):
        for row in range(0, rows, 16):
            for col in range(0, width, 128):
                halves = ([], [])
                for top in (row, row + 8):
                    offset = 65599 * (col // 32) + 131071 * top
                    f = [factor(bases[n], offset) for n in range(5)]
                    later = (f[2] * f[3] * f[4]) * (2.0**-76)
                    for pair in range(2):
                        halves[pair].append(f[pair] * later - 1.0)
                for pair in range(2):
                    block = jnp.concatenate(halves[pair], axis=0).astype(jnp.bfloat16)
                    out_ref[pair, row : row + 16, col : col + 128] = block

    for part in range(2):
        fill(outs[part], [base_ref[part, n] for n in range(5)])


def factors(place, words, rows_all, width):
    rows = rows_all // OWNERS
    spec = pl.BlockSpec((2, rows, width), lambda i, p: (0, i, 0))
    shape = jax.ShapeDtypeStruct((2, rows_all, width), jnp.bfloat16)
    return pl.pallas_call(
        factor_kernel,
        grid_spec=pltpu.PrefetchScalarGridSpec(
            num_scalar_prefetch=1,
            grid=(OWNERS,),
            in_specs=[pl.BlockSpec(words.shape, lambda i, p: (0, 0))],
            out_specs=[spec, spec],
            scratch_shapes=[pltpu.VMEM((2, 5, 8, 128), jnp.int32)],
        ),
        out_shape=[shape, shape],
        compiler_params=pltpu.CompilerParams(vmem_limit_bytes=8 * 2**20),
        cost_estimate=pl.CostEstimate(
            flops=20000 * rows_all * width, bytes_accessed=4 * rows_all * width * 2, transcendentals=0
        ),
    )(place, words)


def product(left, right):
    return lax.dot_general(left, right, (((0,), (0,)), ((), ())), preferred_element_type=jnp.float32)


def early_kernel(place, h0, h1, h3, g0, g1, g3, fa_ref, fb_ref, outa_ref, outb_ref):
    rows_all, width = outa_ref.shape
    rows = rows_all // SIDE

    def block(at, carry):
        here = pl.ds(pl.multiple_of(at * rows, rows), rows)
        both = jnp.concatenate([h1[:, here], h3[:, here]], axis=0)
        for part, (f_ref, out_ref) in enumerate(((fa_ref, outa_ref), (fb_ref, outb_ref))):
            cut = pl.ds(pl.multiple_of(place[6 + part] * width, width), width)
            mine = pl.ds(pl.multiple_of(place[4 + part] * width, width), width)
            near = product(h0[:, here], g0[:, mine])
            far = product(both, jnp.concatenate([g1[:, cut], g3[:, cut]], axis=0))
            near = near + near * f_ref[0, here, :].astype(jnp.float32)
            out_ref[here, :] = near + (far + far * f_ref[1, here, :].astype(jnp.float32))
        return carry

    lax.fori_loop(0, SIDE, block, 0, unroll=True)


def late_kernel(place, h2a, h2b, g2, f_ref, more_ref, out_ref, *, part):
    rows_all, width = more_ref.shape
    rows = rows_all // SIDE
    cell_rows, cell_width = out_ref.shape[1:]
    cut = pl.ds(pl.multiple_of(place[6 + part] * width, width), width)

    def block(at, carry):
        here = pl.ds(pl.multiple_of(at * rows, rows), rows)
        left = jnp.concatenate([h2a[:, here], h2b[:, here]], axis=0)
        value = product(left, g2[:, cut])
        value = value + value * f_ref[0, here, :].astype(jnp.float32) + more_ref[here, :]
        value = value.astype(jnp.bfloat16)
        for x in range(SIDE):
            for side in range(2):
                cell = value[x * cell_rows : (x + 1) * cell_rows, side * cell_width : (side + 1) * cell_width]
                out_ref[(at * SIDE + x) * 2 + side] = cell
        return carry

    lax.fori_loop(0, SIDE, block, 0, unroll=True)


def in_vmem(body, place, args, shape, flops):
    return pl.pallas_call(
        body,
        in_specs=[pl.BlockSpec(memory_space=pltpu.SMEM)] + [pl.BlockSpec(memory_space=pltpu.VMEM)] * len(args),
        out_specs=jax.tree.map(lambda _: pl.BlockSpec(memory_space=pltpu.VMEM), shape),
        out_shape=shape,
        compiler_params=pltpu.CompilerParams(vmem_limit_bytes=24 * 2**20),
        cost_estimate=pl.CostEstimate(flops=flops, bytes_accessed=2**22, transcendentals=0),
    )(place, *args)


def early(place, h, g, scale):
    tokens, rows_all = h[0].shape
    width = scale[0].shape[2]
    shape = jax.ShapeDtypeStruct((rows_all, width), jnp.float32)
    return in_vmem(early_kernel, place, [*h, *g, *scale], [shape, shape], 12 * rows_all * tokens * width)


def late(place, h, g, scale, more, part):
    rows_all, width = more.shape

    def body(*refs):
        late_kernel(*refs, part=part)

    shape = jax.ShapeDtypeStruct((2 * OWNERS, rows_all // OWNERS, width // 2), jnp.bfloat16)
    return in_vmem(body, place, [*h, g, scale, more], shape, 8 * rows_all * g.shape[0] * width)


def weave_kernel(place, blocks_ref, out_ref):
    width = blocks_ref.shape[3]
    for z1, z0, core, low in itertools.product(range(2), repeat=4):
        first = (((z1 * 2 + low) * 2 + core) * 2 + z0) * width
        out_ref[:, first : first + width] = blocks_ref[z1 * 4 + z0 * 2 + core, low]


def weave(place, blocks, columns):
    rows, width = blocks.shape[2:]
    shape = jax.ShapeDtypeStruct((rows, columns), blocks.dtype)
    return in_vmem(weave_kernel, place, [blocks], shape, 1)


def exchange(blocks, axes):
    return lax.all_to_all(blocks, axes, 0, 0, tiled=True)


def added(blocks, axis=0):
    return jnp.sum(blocks.astype(jnp.float32), axis=axis).astype(jnp.bfloat16)


def along_y(block, step):
    return lax.ppermute(block, "y", [(at, (at + step) % SIDE) for at in range(SIDE)])


def per_device(hidden, grad_out, seed_table):
    x, y, core = lax.axis_index("x"), lax.axis_index("y"), lax.axis_index("core")
    tokens, columns = grad_out.shape[1:]
    quarter = columns // SIDE
    half = quarter // 2
    words = exchange(jnp.tile(seed_table[0, 0], (OWNERS, 4)), ("y", "x"))
    other = 1 - core
    groups = half // 32
    place = [x, y, (y * 2 + other) * groups, (y * 2 + core) * groups, y * 2 + other, y * 2 + core, other, core]
    place = jnp.stack(place).astype(jnp.int32)

    h_own = hidden[0]
    h_low = along_y(h_own, 1)
    h_high = along_y(h_own, -1)
    h_facing_a = along_y(h_low[: tokens // 2], 1)
    h_facing_b = along_y(h_high[tokens // 2 :], -1)
    def quarter_for(step):
        return lax.dynamic_slice_in_dim(grad_out[0], (y + step) % SIDE * quarter, quarter, 1)

    g_low, g_high, g_facing = (along_y(quarter_for(step), step) for step in (1, -1, 2))

    rows_all = h_own.shape[1]
    scale = factors(place, words, rows_all, half)
    three = early(place, [h_own, h_high, h_low], [grad_out[0], g_high, g_low], scale)
    facing = [h_facing_a, h_facing_b]
    sent = late(place, facing, g_facing, scale[0], three[0], 0)
    received = lax.ppermute(sent, "core", SWAP)
    both = late(place, facing, g_facing, scale[1], three[1], 1).astype(jnp.float32) + received.astype(jnp.float32)

    got = exchange(both.astype(jnp.bfloat16), ("y", "x", "z0"))
    owned = added(got.reshape(SIDE, 2 * SIDE, *got.shape[1:]), 1)
    near = added(exchange(owned, "z1").reshape(2, 2, *got.shape[1:]))
    total = added(lax.all_gather(near, "zh"))
    return weave(place, lax.all_gather(total, ("z1", "z0", "core")), columns)[None]


def solution(mesh):
    devices = mesh.devices
    zero, dp = devices.shape
    names = ("y", "x", "zh", "z1", "z0", "core")
    split = Mesh(devices.reshape(SIDE, zero // SIDE, dp // 8, 2, 2, 2), names)
    dp_parts = ("zh", "z1", "z0", "core")
    return jax.shard_map(
        per_device,
        mesh=split,
        in_specs=(
            P(dp_parts, ("y", "x"), None),
            P(dp_parts, ("y", "x"), None),
            P(dp_parts, ("y", "x"), None, None),
        ),
        out_specs=P(None, ("y", "x"), None),
        check_vma=False,
    )
```

```python
import itertools

import jax
import jax.numpy as jnp
from jax import lax
from jax.experimental import pallas as pl
from jax.experimental.pallas import tpu as pltpu
from jax.sharding import Mesh, PartitionSpec as P

SWAP = [(0, 1), (1, 0)]
MIX = 73244475
SIDE = 4
OWNERS = SIDE * SIDE


def factor(base, offset):
    k = base + offset
    k = k ^ lax.shift_right_logical(k, 16)
    k = k * MIX
    k = k ^ lax.shift_right_logical(k, 16)
    k = k * MIX
    k = (k ^ lax.shift_right_logical(k, 16)) & 65535
    return k.astype(jnp.float32) + 491520.0


def factor_kernel(place, words_ref, *refs):
    outs, base_ref = refs[:2], refs[2]
    owner = pl.program_id(0)
    x, y = place[0], place[1]
    owner_y, owner_x = owner >> 2, owner & 3
    rows, width = outs[0].shape[1:]
    lane = lax.broadcasted_iota(jnp.int32, (8, 128), 1)
    sub = lax.broadcasted_iota(jnp.int32, (8, 128), 0)
    shared = 65599 * (lane >> 5) + 131071 * sub + 131071 * rows * owner
    keepers = (
        (((owner_y & 2) | (y & 1)) * 4 + x, 0),
        (((owner_y & 2) | (1 - (y & 1))) * 4 + x, 0),
        (owner_y * 4 + x, 1),
        (owner_y * 4 + ((owner_x & 2) | (x & 1)), 2),
        (owner, 3),
    )
    for at, (keeper, step) in enumerate(keepers):
        base = words_ref[pl.ds(keeper, 1), :] + shared + 7919 * step
        for part in range(2):
            base_ref[part, at] = base + 65599 * place[2 + part]

    def fill(out_ref, bases):
        for row in range(0, rows, 16):
            for col in range(0, width, 128):
                halves = ([], [])
                for top in (row, row + 8):
                    offset = 65599 * (col // 32) + 131071 * top
                    f = [factor(bases[n], offset) for n in range(5)]
                    later = (f[2] * f[3] * f[4]) * (2.0**-76)
                    for pair in range(2):
                        halves[pair].append(f[pair] * later - 1.0)
                for pair in range(2):
                    block = jnp.concatenate(halves[pair], axis=0).astype(jnp.bfloat16)
                    out_ref[pair, row : row + 16, col : col + 128] = block

    for part in range(2):
        fill(outs[part], [base_ref[part, n] for n in range(5)])


def factors(place, words, rows_all, width):
    rows = rows_all // OWNERS
    spec = pl.BlockSpec((2, rows, width), lambda i, p: (0, i, 0))
    shape = jax.ShapeDtypeStruct((2, rows_all, width), jnp.bfloat16)
    return pl.pallas_call(
        factor_kernel,
        grid_spec=pltpu.PrefetchScalarGridSpec(
            num_scalar_prefetch=1,
            grid=(OWNERS,),
            in_specs=[pl.BlockSpec(words.shape, lambda i, p: (0, 0))],
            out_specs=[spec, spec],
            scratch_shapes=[pltpu.VMEM((2, 5, 8, 128), jnp.int32)],
        ),
        out_shape=[shape, shape],
        compiler_params=pltpu.CompilerParams(vmem_limit_bytes=8 * 2**20),
        cost_estimate=pl.CostEstimate(
            flops=20000 * rows_all * width, bytes_accessed=4 * rows_all * width * 2, transcendentals=0
        ),
    )(place, words)


def product(left, right):
    return lax.dot_general(left, right, (((0,), (0,)), ((), ())), preferred_element_type=jnp.float32)


def early_kernel(place, h0, h1, h3, g0, g1, g3, fa_ref, fb_ref, outa_ref, outb_ref):
    rows_all, width = outa_ref.shape
    rows = rows_all // SIDE

    def block(at, carry):
        here = pl.ds(pl.multiple_of(at * rows, rows), rows)
        both = jnp.concatenate([h1[:, here], h3[:, here]], axis=0)
        for part, (f_ref, out_ref) in enumerate(((fa_ref, outa_ref), (fb_ref, outb_ref))):
            cut = pl.ds(pl.multiple_of(place[6 + part] * width, width), width)
            mine = pl.ds(pl.multiple_of(place[4 + part] * width, width), width)
            near = product(h0[:, here], g0[:, mine])
            far = product(both, jnp.concatenate([g1[:, cut], g3[:, cut]], axis=0))
            near = near + near * f_ref[0, here, :].astype(jnp.float32)
            out_ref[here, :] = near + (far + far * f_ref[1, here, :].astype(jnp.float32))
        return carry

    lax.fori_loop(0, SIDE, block, 0, unroll=True)


def late_kernel(place, h2a, h2b, g2, f_ref, more_ref, out_ref, *, part):
    rows_all, width = more_ref.shape
    rows = rows_all // SIDE
    cell_rows, cell_width = out_ref.shape[1:]
    cut = pl.ds(pl.multiple_of(place[6 + part] * width, width), width)

    def block(at, carry):
        here = pl.ds(pl.multiple_of(at * rows, rows), rows)
        left = jnp.concatenate([h2a[:, here], h2b[:, here]], axis=0)
        value = product(left, g2[:, cut])
        value = value + value * f_ref[0, here, :].astype(jnp.float32) + more_ref[here, :]
        value = value.astype(jnp.bfloat16)
        for x in range(SIDE):
            for side in range(2):
                cell = value[x * cell_rows : (x + 1) * cell_rows, side * cell_width : (side + 1) * cell_width]
                out_ref[(at * SIDE + x) * 2 + side] = cell
        return carry

    lax.fori_loop(0, SIDE, block, 0, unroll=True)


def in_vmem(body, place, args, shape, flops):
    return pl.pallas_call(
        body,
        in_specs=[pl.BlockSpec(memory_space=pltpu.SMEM)] + [pl.BlockSpec(memory_space=pltpu.VMEM)] * len(args),
        out_specs=jax.tree.map(lambda _: pl.BlockSpec(memory_space=pltpu.VMEM), shape),
        out_shape=shape,
        compiler_params=pltpu.CompilerParams(vmem_limit_bytes=24 * 2**20),
        cost_estimate=pl.CostEstimate(flops=flops, bytes_accessed=2**22, transcendentals=0),
    )(place, *args)


def early(place, h, g, scale):
    tokens, rows_all = h[0].shape
    width = scale[0].shape[2]
    shape = jax.ShapeDtypeStruct((rows_all, width), jnp.float32)
    return in_vmem(early_kernel, place, [*h, *g, *scale], [shape, shape], 12 * rows_all * tokens * width)


def late(place, h, g, scale, more, part):
    rows_all, width = more.shape

    def body(*refs):
        late_kernel(*refs, part=part)

    shape = jax.ShapeDtypeStruct((2 * OWNERS, rows_all // OWNERS, width // 2), jnp.bfloat16)
    return in_vmem(body, place, [*h, g, scale, more], shape, 8 * rows_all * g.shape[0] * width)


def weave_kernel(place, blocks_ref, out_ref):
    width = blocks_ref.shape[3]
    for z1, z0, core, low in itertools.product(range(2), repeat=4):
        first = (((z1 * 2 + low) * 2 + core) * 2 + z0) * width
        out_ref[:, first : first + width] = blocks_ref[z1 * 4 + z0 * 2 + core, low]


def weave(place, blocks, columns):
    rows, width = blocks.shape[2:]
    shape = jax.ShapeDtypeStruct((rows, columns), blocks.dtype)
    return in_vmem(weave_kernel, place, [blocks], shape, 1)


def exchange(blocks, axes):
    return lax.all_to_all(blocks, axes, 0, 0, tiled=True)


def added(blocks, axis=0):
    return jnp.sum(blocks.astype(jnp.float32), axis=axis).astype(jnp.bfloat16)


def along_y(block, step):
    return lax.ppermute(block, "y", [(at, (at + step) % SIDE) for at in range(SIDE)])


def per_device(hidden, grad_out, seed_table):
    x, y, core = lax.axis_index("x"), lax.axis_index("y"), lax.axis_index("core")
    tokens, columns = grad_out.shape[1:]
    quarter = columns // SIDE
    half = quarter // 2
    words = exchange(jnp.tile(seed_table[0, 0], (OWNERS, 4)), ("y", "x"))
    other = 1 - core
    groups = half // 32
    place = [x, y, (y * 2 + other) * groups, (y * 2 + core) * groups, y * 2 + other, y * 2 + core, other, core]
    place = jnp.stack(place).astype(jnp.int32)

    h_own = hidden[0]
    h_low = along_y(h_own, 1)
    h_high = along_y(h_own, -1)
    h_facing_a = along_y(h_low[: tokens // 2], 1)
    h_facing_b = along_y(h_high[tokens // 2 :], -1)
    def quarter_for(step):
        return lax.dynamic_slice_in_dim(grad_out[0], (y + step) % SIDE * quarter, quarter, 1)

    g_low, g_high, g_facing = (along_y(quarter_for(step), step) for step in (1, -1, 2))

    rows_all = h_own.shape[1]
    scale = factors(place, words, rows_all, half)
    three = early(place, [h_own, h_high, h_low], [grad_out[0], g_high, g_low], scale)
    facing = [h_facing_a, h_facing_b]
    sent = late(place, facing, g_facing, scale[0], three[0], 0)
    received = lax.ppermute(sent, "core", SWAP)
    both = late(place, facing, g_facing, scale[1], three[1], 1).astype(jnp.float32) + received.astype(jnp.float32)

    got = exchange(both.astype(jnp.bfloat16), ("y", "x", "z0"))
    owned = added(got.reshape(SIDE, 2 * SIDE, *got.shape[1:]), 1)
    z1 = lax.axis_index("z1")
    given = lax.dynamic_slice_in_dim(owned, (1 - z1) * 2, 2, 0)
    kept = lax.dynamic_slice_in_dim(owned, z1 * 2, 2, 0)
    near = added(jnp.stack([kept, lax.ppermute(given, "z1", SWAP)]))
    total = added(lax.all_gather(near, "zh"))
    return weave(place, lax.all_gather(total, ("z1", "z0", "core")), columns)[None]


def solution(mesh):
    devices = mesh.devices
    zero, dp = devices.shape
    names = ("y", "x", "zh", "z1", "z0", "core")
    split = Mesh(devices.reshape(SIDE, zero // SIDE, dp // 8, 2, 2, 2), names)
    dp_parts = ("zh", "z1", "z0", "core")
    return jax.shard_map(
        per_device,
        mesh=split,
        in_specs=(
            P(dp_parts, ("y", "x"), None),
            P(dp_parts, ("y", "x"), None),
            P(dp_parts, ("y", "x"), None, None),
        ),
        out_specs=P(None, ("y", "x"), None),
        check_vma=False,
    )
```

```python
import itertools

import jax
import jax.numpy as jnp
from jax import lax
from jax.experimental import pallas as pl
from jax.experimental.pallas import tpu as pltpu
from jax.sharding import Mesh, PartitionSpec as P

SWAP = [(0, 1), (1, 0)]
MIX = 73244475
SIDE = 4
OWNERS = SIDE * SIDE


def factor(base, offset):
    k = base + offset
    k = k ^ lax.shift_right_logical(k, 16)
    k = k * MIX
    k = k ^ lax.shift_right_logical(k, 16)
    k = k * MIX
    k = (k ^ lax.shift_right_logical(k, 16)) & 65535
    return k.astype(jnp.float32) + 491520.0


def factor_kernel(place, words_ref, *refs):
    outs, base_ref = refs[:2], refs[2]
    owner = pl.program_id(0)
    x, y = place[0], place[1]
    owner_y, owner_x = owner >> 2, owner & 3
    rows, width = outs[0].shape[1:]
    lane = lax.broadcasted_iota(jnp.int32, (8, 128), 1)
    sub = lax.broadcasted_iota(jnp.int32, (8, 128), 0)
    shared = 65599 * (lane >> 5) + 131071 * sub + 131071 * rows * owner
    keepers = (
        (((owner_y & 2) | (y & 1)) * 4 + x, 0),
        (((owner_y & 2) | (1 - (y & 1))) * 4 + x, 0),
        (owner_y * 4 + x, 1),
        (owner_y * 4 + ((owner_x & 2) | (x & 1)), 2),
        (owner, 3),
    )
    for at, (keeper, step) in enumerate(keepers):
        base = words_ref[pl.ds(keeper, 1), :] + shared + 7919 * step
        for part in range(2):
            base_ref[part, at] = base + 65599 * place[2 + part]

    def fill(out_ref, bases):
        for row in range(0, rows, 16):
            for col in range(0, width, 128):
                halves = ([], [])
                for top in (row, row + 8):
                    offset = 65599 * (col // 32) + 131071 * top
                    f = [factor(bases[n], offset) for n in range(5)]
                    later = (f[2] * f[3] * f[4]) * (2.0**-76)
                    for pair in range(2):
                        halves[pair].append(f[pair] * later - 1.0)
                for pair in range(2):
                    block = jnp.concatenate(halves[pair], axis=0).astype(jnp.bfloat16)
                    out_ref[pair, row : row + 16, col : col + 128] = block

    for part in range(2):
        fill(outs[part], [base_ref[part, n] for n in range(5)])


def factors(place, words, rows_all, width):
    rows = rows_all // OWNERS
    spec = pl.BlockSpec((2, rows, width), lambda i, p: (0, i, 0))
    shape = jax.ShapeDtypeStruct((2, rows_all, width), jnp.bfloat16)
    return pl.pallas_call(
        factor_kernel,
        grid_spec=pltpu.PrefetchScalarGridSpec(
            num_scalar_prefetch=1,
            grid=(OWNERS,),
            in_specs=[pl.BlockSpec(words.shape, lambda i, p: (0, 0))],
            out_specs=[spec, spec],
            scratch_shapes=[pltpu.VMEM((2, 5, 8, 128), jnp.int32)],
        ),
        out_shape=[shape, shape],
        compiler_params=pltpu.CompilerParams(vmem_limit_bytes=8 * 2**20),
        cost_estimate=pl.CostEstimate(
            flops=20000 * rows_all * width, bytes_accessed=4 * rows_all * width * 2, transcendentals=0
        ),
    )(place, words)


def product(left, right):
    return lax.dot_general(left, right, (((0,), (0,)), ((), ())), preferred_element_type=jnp.float32)


def early_kernel(place, h0, h1, h3, g0, g1, g3, fa_ref, fb_ref, outa_ref, outb_ref):
    rows_all, width = outa_ref.shape
    rows = rows_all // SIDE

    def block(at, carry):
        here = pl.ds(pl.multiple_of(at * rows, rows), rows)
        both = jnp.concatenate([h1[:, here], h3[:, here]], axis=0)
        for part, (f_ref, out_ref) in enumerate(((fa_ref, outa_ref), (fb_ref, outb_ref))):
            cut = pl.ds(pl.multiple_of(place[6 + part] * width, width), width)
            mine = pl.ds(pl.multiple_of(place[4 + part] * width, width), width)
            near = product(h0[:, here], g0[:, mine])
            far = product(both, jnp.concatenate([g1[:, cut], g3[:, cut]], axis=0))
            near = near + near * f_ref[0, here, :].astype(jnp.float32)
            out_ref[here, :] = near + (far + far * f_ref[1, here, :].astype(jnp.float32))
        return carry

    lax.fori_loop(0, SIDE, block, 0, unroll=True)


def late_kernel(place, h2a, h2b, g2, f_ref, more_ref, out_ref, *, part):
    rows_all, width = more_ref.shape
    rows = rows_all // SIDE
    cell_rows, cell_width = out_ref.shape[1:]
    cut = pl.ds(pl.multiple_of(place[6 + part] * width, width), width)

    def block(at, carry):
        here = pl.ds(pl.multiple_of(at * rows, rows), rows)
        left = jnp.concatenate([h2a[:, here], h2b[:, here]], axis=0)
        value = product(left, g2[:, cut])
        value = value + value * f_ref[0, here, :].astype(jnp.float32) + more_ref[here, :]
        value = value.astype(jnp.bfloat16)
        for x in range(SIDE):
            for side in range(2):
                cell = value[x * cell_rows : (x + 1) * cell_rows, side * cell_width : (side + 1) * cell_width]
                out_ref[(at * SIDE + x) * 2 + side] = cell
        return carry

    lax.fori_loop(0, SIDE, block, 0, unroll=True)


def in_vmem(body, place, args, shape, flops):
    return pl.pallas_call(
        body,
        in_specs=[pl.BlockSpec(memory_space=pltpu.SMEM)] + [pl.BlockSpec(memory_space=pltpu.VMEM)] * len(args),
        out_specs=jax.tree.map(lambda _: pl.BlockSpec(memory_space=pltpu.VMEM), shape),
        out_shape=shape,
        compiler_params=pltpu.CompilerParams(vmem_limit_bytes=24 * 2**20),
        cost_estimate=pl.CostEstimate(flops=flops, bytes_accessed=2**22, transcendentals=0),
    )(place, *args)


def early(place, h, g, scale):
    tokens, rows_all = h[0].shape
    width = scale[0].shape[2]
    shape = jax.ShapeDtypeStruct((rows_all, width), jnp.float32)
    return in_vmem(early_kernel, place, [*h, *g, *scale], [shape, shape], 12 * rows_all * tokens * width)


def late(place, h, g, scale, more, part):
    rows_all, width = more.shape

    def body(*refs):
        late_kernel(*refs, part=part)

    shape = jax.ShapeDtypeStruct((2 * OWNERS, rows_all // OWNERS, width // 2), jnp.bfloat16)
    return in_vmem(body, place, [*h, g, scale, more], shape, 8 * rows_all * g.shape[0] * width)


def weave_kernel(place, blocks_ref, out_ref):
    width = blocks_ref.shape[3]
    for z1, z0, core, low in itertools.product(range(2), repeat=4):
        first = (((z1 * 2 + low) * 2 + core) * 2 + z0) * width
        out_ref[:, first : first + width] = blocks_ref[z1 * 4 + z0 * 2 + core, low]


def weave(place, blocks, columns):
    rows, width = blocks.shape[2:]
    shape = jax.ShapeDtypeStruct((rows, columns), blocks.dtype)
    return in_vmem(weave_kernel, place, [blocks], shape, 1)


def spread_kernel(seeds_ref, out_ref):
    row = jnp.concatenate([seeds_ref[...]] * (128 // seeds_ref.shape[1]), axis=1)
    out_ref[...] = jnp.broadcast_to(row, out_ref.shape)


def spread(seeds):
    return pl.pallas_call(
        spread_kernel,
        in_specs=[pl.BlockSpec(memory_space=pltpu.VMEM)],
        out_specs=pl.BlockSpec(memory_space=pltpu.VMEM),
        out_shape=jax.ShapeDtypeStruct((OWNERS, 128), seeds.dtype),
        compiler_params=pltpu.CompilerParams(vmem_limit_bytes=2**20),
    )(seeds)


def exchange(blocks, axes):
    return lax.all_to_all(blocks, axes, 0, 0, tiled=True)


def added(blocks, axis=0):
    return jnp.sum(blocks.astype(jnp.float32), axis=axis).astype(jnp.bfloat16)


def along_y(block, step):
    return lax.ppermute(block, "y", [(at, (at + step) % SIDE) for at in range(SIDE)])


def per_device(hidden, grad_out, seed_table):
    x, y, core = lax.axis_index("x"), lax.axis_index("y"), lax.axis_index("core")
    tokens, columns = grad_out.shape[1:]
    quarter = columns // SIDE
    half = quarter // 2
    words = exchange(spread(seed_table[0, 0]), ("y", "x"))
    other = 1 - core
    groups = half // 32
    place = [x, y, (y * 2 + other) * groups, (y * 2 + core) * groups, y * 2 + other, y * 2 + core, other, core]
    place = jnp.stack(place).astype(jnp.int32)

    h_own = hidden[0]
    h_low = along_y(h_own, 1)
    h_high = along_y(h_own, -1)
    h_facing_a = along_y(h_low[: tokens // 2], 1)
    h_facing_b = along_y(h_high[tokens // 2 :], -1)
    def quarter_for(step):
        return lax.dynamic_slice_in_dim(grad_out[0], (y + step) % SIDE * quarter, quarter, 1)

    g_low, g_high, g_facing = (along_y(quarter_for(step), step) for step in (1, -1, 2))

    rows_all = h_own.shape[1]
    scale = factors(place, words, rows_all, half)
    three = early(place, [h_own, h_high, h_low], [grad_out[0], g_high, g_low], scale)
    facing = [h_facing_a, h_facing_b]
    sent = late(place, facing, g_facing, scale[0], three[0], 0)
    received = lax.ppermute(sent, "core", SWAP)
    both = late(place, facing, g_facing, scale[1], three[1], 1).astype(jnp.float32) + received.astype(jnp.float32)

    got = exchange(both.astype(jnp.bfloat16), ("y", "x", "z0"))
    owned = added(got.reshape(SIDE, 2 * SIDE, *got.shape[1:]), 1)
    near = added(exchange(owned, "z1").reshape(2, 2, *got.shape[1:]))
    total = added(lax.all_gather(near, "zh"))
    return weave(place, lax.all_gather(total, ("z1", "z0", "core")), columns)[None]


def solution(mesh):
    devices = mesh.devices
    zero, dp = devices.shape
    names = ("y", "x", "zh", "z1", "z0", "core")
    split = Mesh(devices.reshape(SIDE, zero // SIDE, dp // 8, 2, 2, 2), names)
    dp_parts = ("zh", "z1", "z0", "core")
    return jax.shard_map(
        per_device,
        mesh=split,
        in_specs=(
            P(dp_parts, ("y", "x"), None),
            P(dp_parts, ("y", "x"), None),
            P(dp_parts, ("y", "x"), None, None),
        ),
        out_specs=P(None, ("y", "x"), None),
        check_vma=False,
    )
```
